128 devices in a mesh: ctx: 4 (over x_hi, core), wt: 32 (over z, x_lo, y).
Axes of the slice: x: 4 (x_hi: 2, x_lo: 2; x = x_hi * 2 + x_lo), y: 4, z: 4, core: 2. Of those that a mesh axis runs over, the one named last changes fastest.
Arguments:
- context_x: bfloat16 [4096, 8192], P('ctx'), may hold values from -16 to 16
- query_x: bfloat16 [1024, 8192], P(('ctx', 'wt')), may hold values from -16 to 16
- w_query: bfloat16 [8192, 4096], P('wt'), may hold values from -0.0625 to 0.0625
- key_value_weight: bfloat16 [8192, 1024], P('wt'), may hold values from -0.0625 to 0.0625
Outputs:
- context_out: bfloat16 [4096, 4096], P('ctx', 'wt')
- query_out: bfloat16 [1024, 4096], P('ctx', 'wt')
The draws below stay inside these ranges and needn't reach their ends.
All inputs are finite; a program needn't handle non-finite values.
Results may differ from the reference program's by a relative error of at most 0.018.
The reference program's roundings to bfloat16 on the way (of `cq`) count: a program that leaves them out, or rounds other values in their place, can miss the bound.
Values may be sent and summed in bfloat16 or wider, within the bound.
A program may use at most 128 MiB of HBM per device.

```python
import math
import jax
import jax.numpy as jnp
from jax import lax

MODEL_WIDTH = 8192
HEAD_SIZE = 128
HQ = 32
KEY_VALUE_HEADS = 4
GROUP = 8
BLOCK = 1024
TOKENS = 4096
QN = 1024
N_CTX = 4


def draw_context_x(key, part):
    key = jax.random.fold_in(key, 11)
    value_key = jax.random.fold_in(key, 0)
    return jax.random.truncated_normal(value_key, -5.0, 5.0, (TOKENS, MODEL_WIDTH), jnp.float32).astype(jnp.bfloat16)


def draw_query_x(key, part):
    key = jax.random.fold_in(key, 12)
    value_key = jax.random.fold_in(key, 0)
    return jax.random.truncated_normal(value_key, -5.0, 5.0, (QN, MODEL_WIDTH), jnp.float32).astype(jnp.bfloat16)


def steps_of(own_key, dims, cuts, low, high):
    level, own = 1.0, jax.random.fold_in(own_key, 6)
    for dim, blocks in cuts:
        draws = jnp.exp(jax.random.uniform(jax.random.fold_in(own, dim), (blocks,), jnp.float32, low / len(cuts), high / len(cuts)))
        level = level * jnp.repeat(draws, dims[dim] // blocks).reshape([-1 if axis == dim else 1 for axis in range(len(dims))])
    return level


def bell_draw(key, extent, spread, most, pieces=(), kind=jnp.bfloat16):
    result = spread * jax.random.normal(key, extent, jnp.float32)
    if pieces:
        result = result * steps_of(key, extent, pieces, -0.22, 0.18)
    return jnp.clip(result, -most, most).astype(kind)


def setup_inputs(seed: int = 0) -> dict:
    seeds = jax.random.split(jax.random.key(seed), 5)
    return {
        "context_x": draw_context_x(jax.random.fold_in(seeds[4], 71), 0),
        "query_x": draw_query_x(jax.random.fold_in(seeds[4], 71), 0),
        "w_query": bell_draw(seeds[2], (MODEL_WIDTH, HQ * HEAD_SIZE), MODEL_WIDTH ** -0.5, 0.0625, ((0, 32),)),
        "key_value_weight": bell_draw(seeds[3], (MODEL_WIDTH, 2 * KEY_VALUE_HEADS * HEAD_SIZE), MODEL_WIDTH ** -0.5, 0.0625, ((0, 32),)),
    }


rope_base = 500000.0

def apply_rotation(projected, token_positions):
    token_rows = projected.shape[0]
    heads = projected.shape[1] // HEAD_SIZE
    half = HEAD_SIZE // 2
    shaped = projected.reshape(token_rows, heads, HEAD_SIZE)
    frequency = jnp.exp(-math.log(rope_base) * (2.0 * jnp.arange(half, dtype=jnp.float32) / HEAD_SIZE))
    angle = token_positions.astype(jnp.float32)[:, None] * frequency[None, :]
    cosine = jnp.cos(angle)[:, None, :]
    sine_part = jnp.sin(angle)[:, None, :]
    lower_half = shaped[:, :, :half]
    upper_half = shaped[:, :, half:]
    turned = jnp.concatenate([lower_half * cosine - upper_half * sine_part, upper_half * cosine + lower_half * sine_part], axis=2)
    return turned.reshape(token_rows, heads * HEAD_SIZE)

def rounded(weights):
    return lax.optimization_barrier(weights.astype(jnp.bfloat16)).astype(jnp.float32)

def project(input_rows, w_query, key_value_weight, token_positions):
    token_rows = input_rows.shape[0]
    queries = apply_rotation(jnp.dot(input_rows, w_query, preferred_element_type=jnp.float32), token_positions).astype(jnp.bfloat16)
    paired_halves = jnp.dot(input_rows, key_value_weight, preferred_element_type=jnp.float32).reshape(token_rows, KEY_VALUE_HEADS, 2 * HEAD_SIZE)
    key_rows = apply_rotation(paired_halves[:, :, :HEAD_SIZE].reshape(token_rows, KEY_VALUE_HEADS * HEAD_SIZE), token_positions).astype(jnp.bfloat16).reshape(token_rows, KEY_VALUE_HEADS, HEAD_SIZE)
    values = paired_halves[:, :, HEAD_SIZE:].astype(jnp.bfloat16)
    return (queries, key_rows, values)

def reference(context_x, query_x, w_query, key_value_weight):
    scale = 1.0 / math.sqrt(HEAD_SIZE)
    context_pos = jnp.arange(TOKENS, dtype=jnp.int32)
    query_pos = TOKENS + jnp.arange(QN, dtype=jnp.int32)
    cq, ck, cv = project(context_x, w_query, key_value_weight, context_pos)
    qq, qk, qv = project(query_x, w_query, key_value_weight, query_pos)
    causal = jnp.arange(BLOCK)[:, None] >= jnp.arange(BLOCK)[None, :]
    anchor_ok = jnp.arange(N_CTX)[:, None, None] > 0
    query_causal = jnp.arange(QN)[:, None] >= jnp.arange(QN)[None, :]

    def context_head(head):
        group = head // GROUP
        q_head = lax.dynamic_slice_in_dim(cq, head * HEAD_SIZE, HEAD_SIZE, 1).reshape(N_CTX, BLOCK, HEAD_SIZE).astype(jnp.float32)
        k_group = lax.dynamic_index_in_dim(ck, group, 1, keepdims=False).reshape(N_CTX, BLOCK, HEAD_SIZE).astype(jnp.float32)
        v_group = lax.dynamic_index_in_dim(cv, group, 1, keepdims=False).reshape(N_CTX, BLOCK, HEAD_SIZE).astype(jnp.float32)
        s_anchor = jnp.einsum('nqd,kd->nqk', q_head, k_group[0]) * scale
        s_own = jnp.einsum('nqd,nkd->nqk', q_head, k_group) * scale
        s_anchor = jnp.where(anchor_ok, s_anchor, -1e+30)
        s_own = jnp.where(causal[None], s_own, -1e+30)
        top = jnp.maximum(lax.optimization_barrier(jnp.max(s_anchor, axis=2)), lax.optimization_barrier(jnp.max(s_own, axis=2)))
        p_anchor = jnp.exp(s_anchor - top[:, :, None])
        p_own = jnp.exp(s_own - top[:, :, None])
        total = lax.optimization_barrier(jnp.sum(p_anchor, axis=2)) + lax.optimization_barrier(jnp.sum(p_own, axis=2))
        summed = jnp.einsum('nqk,kd->nqd', rounded(p_anchor), v_group[0]) + jnp.einsum('nqk,nkd->nqd', rounded(p_own), v_group)
        return (summed / total[:, :, None]).reshape(TOKENS, HEAD_SIZE)

    def query_head(head):
        group = head // GROUP
        q_head = lax.dynamic_slice_in_dim(qq, head * HEAD_SIZE, HEAD_SIZE, 1).astype(jnp.float32)
        k_context = lax.dynamic_index_in_dim(ck, group, 1, keepdims=False).astype(jnp.float32)
        v_context = lax.dynamic_index_in_dim(cv, group, 1, keepdims=False).astype(jnp.float32)
        k_query = lax.dynamic_index_in_dim(qk, group, 1, keepdims=False).astype(jnp.float32)
        v_query = lax.dynamic_index_in_dim(qv, group, 1, keepdims=False).astype(jnp.float32)
        s_context = jnp.einsum('qd,kd->qk', q_head, k_context) * scale
        s_self = jnp.where(query_causal, jnp.einsum('qd,kd->qk', q_head, k_query) * scale, -1e+30)
        top = jnp.maximum(lax.optimization_barrier(jnp.max(s_context, axis=1)), lax.optimization_barrier(jnp.max(s_self, axis=1)))
        p_context = jnp.exp(s_context - top[:, None])
        p_self = jnp.exp(s_self - top[:, None])
        total = lax.optimization_barrier(jnp.sum(p_context, axis=1)) + lax.optimization_barrier(jnp.sum(p_self, axis=1))
        summed = jnp.einsum('qk,kd->qd', rounded(p_context), v_context) + jnp.einsum('qk,kd->qd', rounded(p_self), v_query)
        return summed / total[:, None]
    heads = jnp.arange(HQ, dtype=jnp.int32)
    context_heads = lax.map(context_head, heads)
    query_heads = lax.map(query_head, heads)
    context_out = jnp.transpose(context_heads, (1, 0, 2)).reshape(TOKENS, HQ * HEAD_SIZE).astype(jnp.bfloat16)
    query_out = jnp.transpose(query_heads, (1, 0, 2)).reshape(QN, HQ * HEAD_SIZE).astype(jnp.bfloat16)
    return (context_out, query_out)
```

```python
import math

import jax
import jax.numpy as jnp
import numpy as np
from jax import lax
from jax.experimental import pallas as pl
from jax.experimental.pallas import tpu as pltpu
from jax.sharding import PartitionSpec as P


BF = jnp.bfloat16
F32 = jnp.float32
D = 128
NS, NY = 8, 4
CTX_ROWS = 1024
Q_ROWS = 256
TOKENS = 4096
POSITIONS = 5120
EXP2_SCALE = math.log2(math.e) / math.sqrt(D)
MESH = pl.DeviceIdType.MESH
VMEM_LIMIT = 56 * 1024 * 1024


def rope_tables():
    half = D // 2
    frequency = 500000.0 ** (-2.0 * np.arange(half) / D)
    angle = np.arange(POSITIONS)[:, None] * frequency[None, :]
    cos, sin = np.cos(angle), np.sin(angle)
    by_row = np.stack([np.concatenate([cos, cos], 1), np.concatenate([-sin, sin], 1)])
    cos_t = np.concatenate([cos.T.reshape(4, 16, POSITIONS), np.ones((1, 16, POSITIONS))])
    sin_t = np.concatenate([sin.T.reshape(4, 16, POSITIONS), np.zeros((1, 16, POSITIONS))])
    return by_row.astype(np.float32), np.stack([cos_t, sin_t]).astype(np.float32)


def nt_dot(a, b):
    return lax.dot_general(a, b, (((1,), (1,)), ((), ())), preferred_element_type=F32)


SENDS = dict(kv1=8, w1=8, a1=4, a2=8, kvt_p=1, kw2=4, kw2_p=1, w1_p=8, w2=32, w2_p=8, c=4,
             kc_y=4, kc_x=4, kc_p=4, kq_y=4, kq_x=4, kq_p=4)
BASE = {}
_n = 0
for _name, _count in SENDS.items():
    BASE[_name] = _n
    _n += _count
SLOTS = _n


def project_kernel(x_hbm, qx, wq_hbm, kvw_hbm, tabq_hbm, tabk_hbm,
                   cq_out, qq_out, kvc_out, kvq_out,
                   x_v, w1, kv1, kv1t, w2, kw2t, kws, asend, a1, a_all, ar, kq, csend, crecv,
                   kvc, kvq, ut, tab_c, tab_q, tab_kc, tab_kq,
                   send_sem, recv_sem, x_sem, tab_sem, out_sem):
    ctx = lax.axis_index("ctx")
    wt = lax.axis_index("wt")
    x_hi, core = ctx // 2, lax.rem(ctx, 2)
    z, x_lo, y = wt // 8, lax.rem(wt // 4, 2), lax.rem(wt, 4)
    s_me = z * 2 + x_lo
    j_me = x_lo * 4 + y
    x_me = x_hi * 2 + x_lo
    partner = (x_hi * 2 + 1 - core, wt)

    def y_at(k):
        return lax.rem(y + k, 4)

    def y_dev(k):
        return (ctx, s_me * 4 + y_at(k))

    def s_at(k):
        z2 = lax.rem(z + k // 2, 4)
        x2 = x_lo if k % 2 == 0 else 1 - x_lo
        return z2 * 2 + x2

    def s_dev(k):
        return (ctx, s_at(k) * 4 + y)

    def x_at(k):
        return lax.rem(x_me + k, 4)

    def x_dev(k):
        x2 = x_at(k)
        return ((x2 // 2) * 2 + core, z * 8 + lax.rem(x2, 2) * 4 + y)

    def rcopy(name, src, dst, slot_send, slot_recv, dev):
        return pltpu.make_async_remote_copy(
            src_ref=src, dst_ref=dst, send_sem=send_sem.at[BASE[name] + slot_send],
            recv_sem=recv_sem.at[BASE[name] + slot_recv], device_id=dev, device_id_type=MESH)

    started = []

    def send(name, src, dst, slot_send, slot_recv, dev):
        copy = rcopy(name, src, dst, slot_send, slot_recv, dev)
        copy.start()
        started.append(copy)

    def arrived(name, dst, slot):
        rcopy(name, dst, dst, 0, slot, partner).wait_recv()

    tabs = [
        pltpu.make_async_copy(tabq_hbm.at[:, pl.ds(pl.multiple_of(ctx * 1024, 1024), 1024)], tab_c, tab_sem.at[0]),
        pltpu.make_async_copy(tabq_hbm.at[:, pl.ds(pl.multiple_of(TOKENS + ctx * 256, 256), 256)], tab_q, tab_sem.at[1]),
        pltpu.make_async_copy(tabk_hbm.at[:, jnp.minimum(j_me, 4), :, pl.ds(pl.multiple_of(ctx * 1024, 1024), 1024)], tab_kc, tab_sem.at[2]),
        pltpu.make_async_copy(tabk_hbm.at[:, jnp.minimum(j_me, 4), :, pl.ds(pl.multiple_of(TOKENS + ctx * 256, 256), 256)], tab_kq, tab_sem.at[3]),
    ]
    x_loads = [
        pltpu.make_async_copy(x_hbm.at[:, pl.ds(s * 1024, 1024)], x_v.at[s], x_sem.at[s])
        for s in range(NS)
    ]
    half_rows = pl.ds(pl.multiple_of(core * 128, 128), 128)

    def kv_cols(s):
        return pl.ds(pl.multiple_of(s * 128, 128), 128)

    def q_cols(s):
        return pl.ds(pl.multiple_of(s * 512, 512), 512)

    own_kv = pltpu.make_async_copy(kvw_hbm.at[half_rows, kv_cols(s_me)], kv1.at[s_me], recv_sem.at[BASE["kv1"] + s_me])
    own_kv.start()
    own_w = pltpu.make_async_copy(wq_hbm.at[half_rows, q_cols(s_me)], w1.at[s_me, core], recv_sem.at[BASE["w1"] + s_me])
    own_w.start()

    barrier = pltpu.get_barrier_semaphore()
    peers = [partner] + [y_dev(k) for k in range(1, 4)] + [s_dev(k) for k in range(1, 8)]
    peers += [((1 - x_hi) * 2 + core, s_me * 4 + y),
              ((1 - x_hi) * 2 + core, (z * 2 + 1 - x_lo) * 4 + y)]
    for dev in peers:
        pl.semaphore_signal(barrier, inc=1, device_id=dev, device_id_type=MESH)

    f = qx[...].astype(F32)
    for yy in range(NY):
        for s in range(NS):
            at = s * 1024 + yy * 256
            tile = jnp.concatenate([f[:, at:at + 128], f[:, at + 128:at + 256]], axis=0)
            asend[yy, s * 16:(s + 1) * 16, :] = tile.astype(BF)
    a1[y] = asend[y]
    pl.semaphore_wait(barrier, len(peers))

    for k in range(1, 8):
        send("kv1", kvw_hbm.at[half_rows, kv_cols(s_at(k))], kv1.at[s_me], k, s_me, s_dev(k))
    for k in range(1, 4):
        send("a1", asend.at[y_at(k)], a1.at[y], k, y, y_dev(k))
    for k in range(1, 8):
        send("w1", wq_hbm.at[half_rows, q_cols(s_at(k))], w1.at[s_me, core], k, s_me, s_dev(k))
    for copy in x_loads:
        copy.start()
    for copy in tabs:
        copy.start()

    own_kv.wait()
    for k in range(1, 8):
        arrived("kv1", kv1.at[s_at(k)], s_at(k))
    for s in range(NS):
        by_col = kv1[s].T
        pairs = jnp.concatenate(
            [by_col[at + 16 * yy:at + 16 * yy + 16] for yy in range(NY) for at in (0, 64)], axis=0)
        kv1t[core, :, s * 128:(s + 1) * 128] = jnp.where(x_lo == 0, pairs, by_col)
    for k in range(1, 4):
        send("kw2", kv1t.at[core, pl.ds(pl.multiple_of(y_at(k) * 32, 32), 32)], kw2t.at[y, core], k, y, y_dev(k))
    send("kvt_p", kv1t.at[core], kv1t.at[core], 0, 0, partner)
    kw2t[y, core] = kv1t[core, pl.ds(pl.multiple_of(y * 32, 32), 32), :]

    for k in range(1, 4):
        arrived("a1", a1.at[y_at(k)], y_at(k))
    for k in range(1, 8):
        send("a2", a1, a_all.at[s_me], k, s_me, s_dev(k))
    a_all[s_me] = a1[...]

    for k in range(8):
        s = s_at(k)
        if k == 0:
            own_w.wait()
        else:
            arrived("w1", w1.at[s, core], s)
        for m in range(1, 4):
            send("w2", w1.at[s, core, :, pl.ds(pl.multiple_of(y_at(m) * 128, 128), 128)],
                 w2.at[s, y, core], k * 4 + m, s * 4 + y, y_dev(m))
        send("w1_p", w1.at[s, core], w1.at[s, core], k, s, partner)
        w2[s, y, core] = w1[s, core, :, pl.ds(pl.multiple_of(y * 128, 128), 128)]

    for k in range(1, 4):
        arrived("kw2", kw2t.at[y_at(k), core], y_at(k))
    send("kw2_p", kw2t.at[:, core], kw2t.at[:, core], 0, 0, partner)
    arrived("kw2_p", kw2t.at[:, 1 - core], 0)

    for s in range(NS):
        for yy in range(NY):
            for h in range(2):
                at = yy * 256 + h * 128
                kws[s, :, at:at + 128] = kw2t[yy, h, :, s * 128:(s + 1) * 128]
    for copy in x_loads:
        copy.wait()
    for copy in tabs:
        copy.wait()

    @pl.loop(0, 4)
    def _(m):
        rows = pl.ds(pl.multiple_of(m * 256, 256), 256)
        total = nt_dot(x_v[0, rows, :], kws[0])
        for s in range(1, NS):
            total = total + nt_dot(x_v[s, rows, :], kws[s])
        ut[:, rows] = total.T

    low, high = ut[0:16, :], ut[16:32, :]
    cos, sin = tab_kc[0], tab_kc[1]
    kvc[ctx, j_me, 0:16, :] = (low * cos - high * sin).astype(BF)
    kvc[ctx, j_me, 16:32, :] = (high * cos + low * sin).astype(BF)
    for k in range(1, 4):
        send("kc_y", kvc.at[ctx, j_me], kvc.at[ctx, j_me], k, y, y_dev(k))

    for k in range(1, 8):
        arrived("a2", a_all.at[s_at(k)], s_at(k))
    for t in range(NS):
        v = a_all[:, :, t * 16:(t + 1) * 16, :].astype(F32).reshape(32, 2, 8, 128)
        ar[:, t * 256:t * 256 + 128] = v[:, 0].reshape(256, 128).astype(BF)
        ar[:, t * 256 + 128:(t + 1) * 256] = v[:, 1].reshape(256, 128).astype(BF)
    arrived("kvt_p", kv1t.at[1 - core], 0)
    for s in range(NS):
        for h in range(2):
            at = s * 256 + h * 128
            kq[:, at:at + 128] = kv1t[h, :, s * 128:(s + 1) * 128]
    for s in range(NS):
        arrived("w1_p", w1.at[s, 1 - core], s)
    kv_part = nt_dot(ar[...], kq[...]).T
    for yy in range(NY):
        csend[yy, 256:288, :] = kv_part[yy * 32:(yy + 1) * 32, 0:128]
        csend[yy, 288:320, :] = kv_part[yy * 32:(yy + 1) * 32, 128:256]

    @pl.loop(0, 2)
    def _(m):
        rows = pl.ds(pl.multiple_of(m * 128, 128), 128)
        part = jnp.dot(ar[rows, :], w1[...].reshape(2048, 512), preferred_element_type=F32)
        for yy in range(NY):
            csend[yy, rows, :] = part[:, yy * 128:(yy + 1) * 128]

    for k in range(1, 4):
        send("c", csend.at[y_at(k)], crecv.at[y], k, y, y_dev(k))
    crecv[y] = csend[y]

    def kv_hop_x(name, buf):
        for k in range(1, 4):
            block = buf.at[ctx, x_lo * 4 + y_at(k)]
            arrived(name + "_y", block, y_at(k))
        mine = buf.at[ctx, pl.ds(x_lo * 4, 4)]
        for k in range(1, 4):
            send(name + "_x", mine, mine, k, x_me, x_dev(k))
        send(name + "_p", mine, mine, 0, x_me, partner)

    def of_x(buf, xs, cc):
        return buf.at[(xs // 2) * 2 + cc, pl.ds(lax.rem(xs, 2) * 4, 4)]

    def kv_hop_core(name, buf):
        for k in range(1, 4):
            block = of_x(buf, x_at(k), core)
            arrived(name + "_x", block, x_at(k))
            send(name + "_p", block, block, k, x_at(k), partner)

    def kv_last(name, buf):
        for k in range(4):
            arrived(name + "_p", of_x(buf, x_at(k), 1 - core), x_at(k))

    kv_hop_x("kc", kvc)

    for k in range(8):
        s = s_at(k)
        for m in range(1, 4):
            arrived("w2", w2.at[s, y_at(m), core], s * 4 + y_at(m))
        send("w2_p", w2.at[s, :, core], w2.at[s, :, core], k, s, partner)

    for k in range(1, 4):
        arrived("c", crecv.at[y_at(k)], y_at(k))
    total = crecv[0] + crecv[1] + crecv[2] + crecv[3]
    u = total[0:256]
    qq_out[...] = (u * tab_q[0] + pltpu.roll(u, 64, 1) * tab_q[1]).astype(BF)
    u = jnp.concatenate([total[256:288], total[288:320]], axis=1)
    low, high = u[0:16], u[16:32]
    cos, sin = tab_kq[0], tab_kq[1]
    kvq[ctx, j_me, 0:16, :] = (low * cos - high * sin).astype(BF)
    kvq[ctx, j_me, 16:32, :] = (high * cos + low * sin).astype(BF)
    for k in range(1, 4):
        send("kq_y", kvq.at[ctx, j_me], kvq.at[ctx, j_me], k, y, y_dev(k))

    kv_hop_core("kc", kvc)
    kv_hop_x("kq", kvq)

    for s in range(NS):
        arrived("w2_p", w2.at[s, :, 1 - core], s)

    @pl.loop(0, 4)
    def _(m):
        rows = pl.ds(pl.multiple_of(m * 256, 256), 256)
        total = jnp.dot(x_v[0, rows, :], w2[0].reshape(1024, D), preferred_element_type=F32)
        for s in range(1, NS):
            total = total + jnp.dot(x_v[s, rows, :], w2[s].reshape(1024, D), preferred_element_type=F32)
        cq_out[rows, :] = (total * tab_c[0, rows, :] + pltpu.roll(total, 64, 1) * tab_c[1, rows, :]).astype(BF)

    kv_hop_core("kq", kvq)
    kv_last("kc", kvc)
    out_c = pltpu.make_async_copy(kvc, kvc_out, out_sem.at[0])
    out_c.start()
    kv_last("kq", kvq)
    out_q = pltpu.make_async_copy(kvq, kvq_out, out_sem.at[1])
    out_q.start()
    for copy in started:
        copy.wait_send()
    out_c.wait()
    out_q.wait()


def project(context_x, query_x, w_query, key_value_weight, by_row, by_column):
    any_spec = pl.BlockSpec(memory_space=pl.ANY)
    vmem = pl.BlockSpec(memory_space=pltpu.VMEM)
    return pl.pallas_call(
        project_kernel,
        out_shape=[
            jax.ShapeDtypeStruct((CTX_ROWS, D), BF),
            jax.ShapeDtypeStruct((Q_ROWS, D), BF),
            jax.ShapeDtypeStruct((4, 8, 32, 1024), BF),
            jax.ShapeDtypeStruct((4, 8, 32, 256), BF),
        ],
        in_specs=[any_spec, vmem, any_spec, any_spec, any_spec, any_spec],
        out_specs=[vmem, vmem, any_spec, any_spec],
        scratch_shapes=[
            pltpu.VMEM((NS, CTX_ROWS, 1024), BF),
            pltpu.VMEM((NS, 2, 128, 512), BF),
            pltpu.VMEM((NS, 128, 128), BF),
            pltpu.VMEM((2, 128, 1024), BF),
            pltpu.VMEM((NS, NY, 2, 128, 128), BF),
            pltpu.VMEM((NY, 2, 32, 1024), BF),
            pltpu.VMEM((NS, 32, 1024), BF),
            pltpu.VMEM((NY, 128, 128), BF),
            pltpu.VMEM((NY, 128, 128), BF),
            pltpu.VMEM((NS, NY, 128, 128), BF),
            pltpu.VMEM((Q_ROWS, 2048), BF),
            pltpu.VMEM((128, 2048), BF),
            pltpu.VMEM((NY, 320, 128), F32),
            pltpu.VMEM((NY, 320, 128), F32),
            pltpu.VMEM((4, 8, 32, 1024), BF),
            pltpu.VMEM((4, 8, 32, 256), BF),
            pltpu.VMEM((32, 1024), F32),
            pltpu.VMEM((2, CTX_ROWS, D), F32),
            pltpu.VMEM((2, Q_ROWS, D), F32),
            pltpu.VMEM((2, 16, 1024), F32),
            pltpu.VMEM((2, 16, 256), F32),
            pltpu.SemaphoreType.DMA((SLOTS,)),
            pltpu.SemaphoreType.DMA((SLOTS,)),
            pltpu.SemaphoreType.DMA((NS,)),
            pltpu.SemaphoreType.DMA((4,)),
            pltpu.SemaphoreType.DMA((2,)),
        ],
        compiler_params=pltpu.CompilerParams(
            collective_id=0, has_side_effects=True, vmem_limit_bytes=VMEM_LIMIT),
        name="project",
    )(context_x, query_x, w_query, key_value_weight, by_row, by_column)


def weights_of(scores):
    top = jnp.max(scores[0], axis=1, keepdims=True)
    for s in scores[1:]:
        top = jnp.maximum(top, jnp.max(s, axis=1, keepdims=True))
    weights = [jnp.exp2((s - top) * EXP2_SCALE) for s in scores]
    total = jnp.sum(weights[0], axis=1, keepdims=True)
    for w in weights[1:]:
        total = total + jnp.sum(w, axis=1, keepdims=True)
    return [w.astype(BF) for w in weights], total


def attend_kernel(cq, qq, kvc, kvq, c_out, q_out, keys, values, qkeys, qvalues):
    ctx = lax.axis_index("ctx")
    for b in range(4):
        keys[b] = jnp.concatenate(
            [kvc[b, j, 0:16, :] for j in range(4)] + [kvc[b, j, 16:32, :] for j in range(4)], axis=0)
        values[b] = kvc[b, 4:8].reshape(128, 1024).T
        qkeys[:, b * 256:(b + 1) * 256] = jnp.concatenate(
            [kvq[b, j, 0:16, :] for j in range(4)] + [kvq[b, j, 16:32, :] for j in range(4)], axis=0)
        qvalues[b * 256:(b + 1) * 256, :] = kvq[b, 4:8].reshape(128, 256).T

    for i in range(4):
        q = cq[i * 256:(i + 1) * 256, :]
        wide = (i + 1) * 256
        s_anchor = jnp.dot(q, keys[0], preferred_element_type=F32)
        s_anchor = jnp.where(ctx > 0, s_anchor, -1e30)
        s_own = jnp.dot(q, keys[ctx, :, 0:wide], preferred_element_type=F32)
        row = lax.broadcasted_iota(jnp.int32, (256, wide), 0) + i * 256
        col = lax.broadcasted_iota(jnp.int32, (256, wide), 1)
        s_own = jnp.where(row >= col, s_own, -1e30)
        (p_anchor, p_own), total = weights_of([s_anchor, s_own])
        out = jnp.dot(p_anchor, values[0], preferred_element_type=F32)
        out = out + jnp.dot(p_own, values[ctx, 0:wide, :], preferred_element_type=F32)
        c_out[i * 256:(i + 1) * 256, :] = (out / total).astype(BF)

    for i in range(2):
        q = qq[i * 128:(i + 1) * 128, :]
        scores = [jnp.dot(q, keys[b], preferred_element_type=F32) for b in range(4)]
        s_self = jnp.dot(q, qkeys[...], preferred_element_type=F32)
        row = lax.broadcasted_iota(jnp.int32, (128, 1024), 0) + (ctx * 256 + i * 128)
        col = lax.broadcasted_iota(jnp.int32, (128, 1024), 1)
        scores.append(jnp.where(row >= col, s_self, -1e30))
        weights, total = weights_of(scores)
        out = jnp.dot(weights[4], qvalues[...], preferred_element_type=F32)
        for b in range(4):
            out = out + jnp.dot(weights[b], values[b], preferred_element_type=F32)
        q_out[i * 128:(i + 1) * 128, :] = (out / total).astype(BF)


def attend(cq, qq, kvc, kvq):
    vmem = pl.BlockSpec(memory_space=pltpu.VMEM)
    return pl.pallas_call(
        attend_kernel,
        out_shape=[jax.ShapeDtypeStruct((CTX_ROWS, D), BF), jax.ShapeDtypeStruct((Q_ROWS, D), BF)],
        in_specs=[vmem] * 4,
        out_specs=[vmem] * 2,
        scratch_shapes=[
            pltpu.VMEM((4, 128, 1024), BF),
            pltpu.VMEM((4, 1024, 128), BF),
            pltpu.VMEM((128, 1024), BF),
            pltpu.VMEM((1024, 128), BF),
        ],
        compiler_params=pltpu.CompilerParams(vmem_limit_bytes=VMEM_LIMIT),
        name="attend",
    )(cq, qq, kvc, kvq)


def per_device(context_x, query_x, w_query, key_value_weight):
    by_row, by_column = rope_tables()
    cq, qq, kvc, kvq = project(
        context_x, query_x, w_query, key_value_weight, jnp.asarray(by_row), jnp.asarray(by_column))
    return tuple(attend(cq, qq, kvc, kvq))


def solution(mesh):
    placed = (P("ctx", None), P(("ctx", "wt"), None), P("wt", None), P("wt", None))
    return jax.shard_map(
        per_device,
        mesh=mesh,
        in_specs=placed,
        out_specs=(P("ctx", "wt"), P("ctx", "wt")),
        check_vma=False,
    )
```

```python
import math

import jax
import jax.numpy as jnp
import numpy as np
from jax import lax
from jax.experimental import pallas as pl
from jax.experimental.pallas import tpu as pltpu
from jax.sharding import PartitionSpec as P


BF = jnp.bfloat16
F32 = jnp.float32
D = 128
NS, NY = 8, 4
CTX_ROWS = 1024
Q_ROWS = 256
TOKENS = 4096
POSITIONS = 5120
EXP2_SCALE = math.log2(math.e) / math.sqrt(D)
MESH = pl.DeviceIdType.MESH
VMEM_LIMIT = 56 * 1024 * 1024


def rope_tables():
    half = D // 2
    frequency = 500000.0 ** (-2.0 * np.arange(half) / D)
    angle = np.arange(POSITIONS)[:, None] * frequency[None, :]
    cos, sin = np.cos(angle), np.sin(angle)
    by_row = np.stack([np.concatenate([cos, cos], 1), np.concatenate([-sin, sin], 1)])
    shape = (1, 4, 16, POSITIONS)
    cos_t = np.concatenate([cos.T.reshape(shape), np.ones(shape)])
    sin_t = np.concatenate([sin.T.reshape(shape), np.zeros(shape)])
    return by_row.astype(np.float32), np.stack([cos_t, sin_t]).astype(np.float32)


def nt_dot(a, b):
    return lax.dot_general(a, b, (((1,), (1,)), ((), ())), preferred_element_type=F32)


SLOTS_OF = dict(kvd=32, kvd_p=4, kv1=16, kv1_p=2, w1=16, a1=16, a2=8, w1_p=16, w2=64, w2_p=16, ck=8, cq=8,
                kc_y=4, kc_x=4, kc_p=4, kq_y=4, kq_x=4, kq_p=1)
BASE = {}
SLOTS = 0
for _name, _count in SLOTS_OF.items():
    BASE[_name] = SLOTS
    SLOTS += _count


def scores_of(q, keys):
    return jnp.dot(q, keys, preferred_element_type=F32)


def attend(scores, values, before=None):
    top = jnp.max(scores[0], axis=1, keepdims=True)
    for s in scores[1:]:
        top = jnp.maximum(top, jnp.max(s, axis=1, keepdims=True))
    if before is not None:
        top = jnp.maximum(top, before[0])
    total = out = None
    for s, v in zip(scores, values):
        w = jnp.exp2((s - top) * EXP2_SCALE)
        t = jnp.sum(w, axis=1, keepdims=True)
        o = jnp.dot(w.astype(BF), v, preferred_element_type=F32)
        total, out = (t, o) if total is None else (total + t, out + o)
    if before is not None:
        shrink = jnp.exp2((before[0] - top) * EXP2_SCALE)
        total = total + before[1] * shrink
        out = out + before[2] * shrink
    return top, total, out


def layer_kernel(x_hbm, qx, wq_hbm, kvw_hbm, tabq_hbm, tabk_hbm, c_out, q_out,
                 x_v, w_src, kv_src, kvt, kva, kws, w1, w2, asend, a1_0, a1_1, a_all, ar,
                 ck_send, ck_recv, cq_send, cq_recv,
                 kvc, kvq, acc, qq, keys, values, qkeys, qvalues, part_m, part_l, part_o,
                 tab_c, tab_q, tab_kc, tab_kq, send_sem, recv_sem, x_sem, tab_sem, load_sem):
    ctx = lax.axis_index("ctx")
    wt = lax.axis_index("wt")
    x_hi, core = ctx // 2, lax.rem(ctx, 2)
    z, x_lo, y = wt // 8, lax.rem(wt // 4, 2), lax.rem(wt, 4)
    x_me = x_hi * 2 + x_lo
    partner = (x_hi * 2 + 1 - core, wt)
    o_me, b_me = (z, y), (y, z)
    so_me = (z * 2 + x_lo, y * 2 + x_lo)

    def plus(a, k):
        return lax.rem(a + k, 4)

    def device(c, z2, x2, y2):
        return (c, z2 * 8 + x2 * 4 + y2)

    def x_side(k):
        return x_lo if k % 2 == 0 else 1 - x_lo

    def so_at(col, k):
        return plus(o_me[col], k // 2) * 2 + x_side(k)

    def so_dev(col, k):
        c2 = ctx if k % 2 == 0 else lax.rem(x_hi + core, 2) * 2 + core
        o2 = plus(o_me[col], k // 2)
        return device(c2, o2, x_side(k), y) if col == 0 else device(c2, z, x_side(k), o2)

    def b_dev(col, k):
        return device(ctx, z, x_lo, plus(y, k)) if col == 0 else device(ctx, plus(z, k), x_lo, y)

    def o_dev(col, k):
        return b_dev(1 - col, k)

    def a1_dev(col, k):
        b2 = plus(b_me[col], k // 2)
        return device(ctx, z, x_side(k), b2) if col == 0 else device(ctx, b2, x_side(k), y)

    def a1_slot(col, x2, b2):
        return col * 8 + (x2 * 4 + b2 if col == 0 else b2 * 2 + x2)

    def a1_at(col, x2, b2):
        return a1_0.at[x2, b2] if col == 0 else a1_1.at[b2, x2]

    def wt_at(k):
        return plus(z, k // 8), x_side(k), plus(y, k // 2)

    def wt_dev(k):
        return device(ctx, *wt_at(k))

    def x_at(k):
        return plus(x_me, k)

    def x_dev(k):
        x2 = x_at(k)
        return device((x2 // 2) * 2 + core, z, lax.rem(x2, 2), y)

    def rcopy(name, src, dst, slot_send, slot_recv, dev):
        return pltpu.make_async_remote_copy(
            src_ref=src, dst_ref=dst, send_sem=send_sem.at[BASE[name] + slot_send],
            recv_sem=recv_sem.at[BASE[name] + slot_recv], device_id=dev, device_id_type=MESH)

    started = []

    def send(name, src, dst, slot_send, slot_recv, dev):
        copy = rcopy(name, src, dst, slot_send, slot_recv, dev)
        copy.start()
        started.append(copy)
        return copy

    def sent(copies):
        for copy in copies:
            copy.wait_send()
        started[:] = [c for c in started if not any(c is copy for copy in copies)]

    def arrived(name, dst, slot):
        rcopy(name, dst, dst, 0, slot, partner).wait_recv()

    def lanes(i, width=128):
        return pl.ds(pl.multiple_of(i * width, width), width)

    load_kv = pltpu.make_async_copy(kvw_hbm, kv_src, load_sem.at[0])
    load_kv.start()
    for o2 in range(4):
        for x2 in range(2):
            for z2 in range(4):
                pltpu.make_async_copy(
                    wq_hbm.at[pl.ds(pl.multiple_of(128 + core * 64, 64), 64), pl.ds((z2 * 8 + x2 * 4 + o2) * 128, 128)],
                    w_src.at[o2 * 2 + x2, :, z2 * 128:(z2 + 1) * 128], load_sem.at[1]).start()
    first_rows = pl.ds(pl.multiple_of(core * 64, 64), 64)
    own_w = pltpu.make_async_copy(wq_hbm.at[first_rows, lanes(so_me[0], 512)], w1.at[0, so_me[0], core], load_sem.at[2])
    own_w.start()
    ctx_rows = pl.ds(pl.multiple_of(ctx * 1024, 1024), 1024)
    query_rows = pl.ds(pl.multiple_of(TOKENS + ctx * 256, 256), 256)
    tabs = [
        pltpu.make_async_copy(tabk_hbm.at[:, x_lo, y, :, ctx_rows], tab_kc, tab_sem.at[2]),
        pltpu.make_async_copy(tabk_hbm.at[:, x_lo, y, :, query_rows], tab_kq, tab_sem.at[3]),
        pltpu.make_async_copy(tabq_hbm.at[:, ctx_rows], tab_c, tab_sem.at[0]),
        pltpu.make_async_copy(tabq_hbm.at[:, query_rows], tab_q, tab_sem.at[1]),
    ]
    x_loads = [
        pltpu.make_async_copy(x_hbm.at[:, pl.ds(s * 1024, 1024)], x_v.at[s], x_sem.at[s])
        for s in range(NS)
    ]

    barrier = pltpu.get_barrier_semaphore()
    peers = [partner] + [x_dev(k) for k in range(1, 4)]
    peers += [wt_dev(k) for k in range(1, 32)]
    for col in range(2):
        peers += [so_dev(col, k) for k in (1, 3, 5, 7)]
    for dev in peers:
        pl.semaphore_signal(barrier, inc=1, device_id=dev, device_id_type=MESH)
    for copy in x_loads + tabs:
        copy.start()

    f = qx[...].astype(F32)
    for col in range(2):
        for bb in range(4):
            for t in range(4):
                at = [t * 2048 + bb * 256, t * 2048 + 1024 + bb * 256] if col == 0 else [
                    bb * 2048 + t * 256 + 128, bb * 2048 + 1024 + t * 256 + 128]
                tile = jnp.concatenate([f[:, c:c + 128] for c in at], axis=0)
                asend[col, bb, t * 16:(t + 1) * 16, :] = tile.astype(BF)
    a1_0[x_lo, y] = asend[0, y]
    a1_1[z, x_lo] = asend[1, z]

    core_cols = pl.ds(pl.multiple_of(core * 16, 16), 16)
    other_cols = pl.ds(pl.multiple_of(16 - core * 16, 16), 16)

    load_kv.wait()
    for g in range(4):
        for x2 in range(2):
            by_col = kv_src[:, g * 256 + x2 * 128:g * 256 + (x2 + 1) * 128].T
            if x2 == 0:
                by_col = jnp.concatenate(
                    [by_col[at + 16 * yy:at + 16 * yy + 16] for yy in range(4) for at in (0, 64)], axis=0)
            kvt[g, x2] = by_col.reshape(4, 32, 256)
    pltpu.make_async_copy(w_src, w_src, load_sem.at[1]).wait()
    w1[1, so_me[1], core] = w_src[so_me[1]]
    kva[0, :, core_cols, lanes(so_me[0])] = kvt[z, x_lo, :, core_cols, 0:128]
    for g in range(4):
        kva[1, g, core_cols, lanes(so_me[1])] = kvt[g, x_lo, y, core_cols, 128:256]
    kws[z, x_lo, y, core] = kvt[z, x_lo, y, :, lanes(core)]
    pl.semaphore_wait(barrier, len(peers))

    def kv_piece(col, k):
        o2 = plus(o_me[col], k // 2)
        if col == 0:
            return kvt.at[o2, x_side(k), :, core_cols, 0:128]
        return kvt.at[:, x_side(k), o2, core_cols, 128:256]

    half_lanes = lanes(core)
    for k in range(1, 32):
        z2, x2, y2 = wt_at(k)
        send("kvd", kvt.at[z2, x2, y2, :, half_lanes], kws.at[z, x_lo, y, core], k, wt, wt_dev(k))
    for k in (2, 6, 3, 7, 4, 5, 1):
        for col in range(2):
            send("a1", asend.at[col, plus(b_me[col], k // 2)], a1_at(col, x_lo, b_me[col]), col * 8 + k,
                 a1_slot(col, x_lo, b_me[col]), a1_dev(col, k))

    def w_piece(col, k):
        if col == 0:
            return wq_hbm.at[first_rows, lanes(so_at(0, k), 512)]
        return w_src.at[so_at(1, k)]

    def w2_at(col, so, b, c):
        o2, x2 = so // 2, lax.rem(so, 2)
        return w2.at[o2, x2, b, 0, c] if col == 0 else w2.at[b, x2, o2, 1, c]

    def w2_row(col, so, c):
        o2, x2 = so // 2, lax.rem(so, 2)
        return w2.at[o2, x2, :, 0, c] if col == 0 else w2.at[:, x2, o2, 1, c]

    def forward_w(col, k):
        so = so_at(col, k)
        if k > 0:
            arrived("w1", w1.at[col, so, core], col * 8 + so)
        for m in range(1, 4):
            send("w2", w1.at[col, so, core, :, lanes(plus(b_me[col], m))], w2_at(col, so, b_me[col], core),
                 (col * 8 + k) * 4 + m, (col * 8 + so) * 4 + b_me[col], b_dev(col, m))
        send("w1_p", w1.at[col, so, core], w1.at[col, so, core], col * 8 + k, col * 8 + so, partner)
        w2_at(col, so, b_me[col], core)[...] = w1[col, so, core, :, lanes(b_me[col])]

    for k in (2, 6, 3, 7, 1, 4, 5):
        for col in range(2):
            send("w1", w_piece(col, k), w1.at[col, so_me[col], core], col * 8 + k, col * 8 + so_me[col], so_dev(col, k))
    own_w.wait()
    for col in range(2):
        forward_w(col, 0)

    for col in range(2):
        for k in range(1, 8):
            x2, b2 = x_side(k), plus(b_me[col], k // 2)
            arrived("a1", a1_at(col, x2, b2), a1_slot(col, x2, b2))
    rows_at = (lambda o2: a_all.at[0, o2], lambda o2: a_all.at[1, :, :, o2])
    for k in (1, 3, 2):
        send("a2", a1_0, rows_at[0](z), k, z, o_dev(0, k))
        send("a2", a1_1, rows_at[1](y), 4 + k, 4 + y, o_dev(1, k))
    a_all[0, z] = a1_0[...]
    for z2 in range(4):
        for x2 in range(2):
            a_all[1, z2, x2, y] = a1_1[z2, x2]

    for k in (2, 6, 3, 7, 4, 5, 1):
        for col in range(2):
            send("kv1", kv_piece(col, k), kva.at[col, :, core_cols, lanes(so_me[col])], col * 8 + k, col * 8 + so_me[col], so_dev(col, k))

    near = (0, 1, 3, 2)
    order = (0, 2, 6, 3, 7, 1, 4, 5)
    for dz in near:
        z2 = plus(z, dz)
        for k in range(8 * dz, 8 * dz + 8):
            if k > 0:
                _, x2, y2 = wt_at(k)
                arrived("kvd", kws.at[z2, x2, y2, core], z2 * 8 + x2 * 4 + y2)
        send("kvd_p", kws.at[z2, :, :, core], kws.at[z2, :, :, core], dz, z2, partner)
    for copy in x_loads + tabs:
        copy.wait()
    u = None
    for dz in near:
        z2 = plus(z, dz)
        arrived("kvd_p", kws.at[z2, :, :, 1 - core], z2)
        for x2 in range(2):
            kw = jnp.concatenate([kws[z2, x2, yy, h] for yy in range(4) for h in range(2)], axis=1)
            part = nt_dot(kw, x_v[z2 * 2 + x2])
            u = part if u is None else u + part
        for k in {1: order[1:3], 3: order[3:5]}.get(dz, ()):
            for col in range(2):
                forward_w(col, k)
    low, high = u[0:16], u[16:32]
    cos, sin = tab_kc[0], tab_kc[1]
    kvc[x_hi, core, x_lo, y, 0:16, :] = (low * cos - high * sin).astype(BF)
    kvc[x_hi, core, x_lo, y, 16:32, :] = (high * cos + low * sin).astype(BF)

    own = kvc.at[x_hi, core, x_lo, y]
    for k in range(1, 4):
        send("kc_y", own, own, k, y, b_dev(0, k))
    for k in order[5:]:
        for col in range(2):
            forward_w(col, k)

    def turn_kc():
        for k in range(1, 4):
            arrived("kc_y", kvc.at[x_hi, core, x_lo, plus(y, k)], plus(y, k))
        row = kvc.at[x_hi, core, x_lo]
        for k in (2, 1, 3):
            send("kc_x", row, row, k, x_me, x_dev(k))
        send("kc_p", row, row, 0, x_me, partner)

    def share_kc():
        for k in (1, 3, 2):
            xs = x_at(k)
            row = kvc.at[xs // 2, core, lax.rem(xs, 2)]
            arrived("kc_x", row, xs)
            send("kc_p", row, row, k, xs, partner)

    def take_kc():
        for k in range(4):
            xs = x_at(k)
            arrived("kc_p", kvc.at[xs // 2, 1 - core, lax.rem(xs, 2)], xs)

    def prepare(c):
        for xh in range(2):
            kv = kvc[xh, c].reshape(8, 32, 1024)
            keys[xh * 2 + c] = jnp.concatenate(
                [kv[j, 0:16] for j in range(4)] + [kv[j, 16:32] for j in range(4)], axis=0)
            values[xh * 2 + c] = kv[4:8].reshape(128, 1024).T

    def turn_kq():
        for k in range(1, 4):
            arrived("kq_y", kvq.at[x_hi, core, x_lo, plus(y, k)], plus(y, k))
        row_y = kvq.at[x_hi, core, x_lo]
        for k in range(1, 4):
            send("kq_x", row_y, row_y, k, x_me, x_dev(k))

    def share_kq():
        for k in range(1, 4):
            xs = x_at(k)
            arrived("kq_x", kvq.at[xs // 2, core, lax.rem(xs, 2)], xs)
        send("kq_p", kvq.at[:, core], kvq.at[:, core], 0, 0, partner)

    def take_kq():
        arrived("kq_p", kvq.at[:, 1 - core], 0)

    def share_w(col, k):
        so = so_at(col, k)
        for m in range(1, 4):
            b2 = plus(b_me[col], m)
            arrived("w2", w2_at(col, so, b2, core), (col * 8 + so) * 4 + b2)
        send("w2_p", w2_row(col, so, core), w2_row(col, so, core), col * 8 + k, col * 8 + so, partner)

    for col in range(2):
        for k in range(1, 8):
            arrived("kv1", kva.at[col, :, core_cols, lanes(so_at(col, k))], col * 8 + so_at(col, k))
        send("kv1_p", kva.at[col, :, core_cols], kva.at[col, :, core_cols], col, col, partner)
    for col in range(2):
        arrived("kv1_p", kva.at[col, :, other_cols], col)
        for k in range(1, 4):
            o2 = plus(o_me[col], k)
            arrived("a2", rows_at[col](o2), col * 4 + o2)
        for t in range(4):
            v = a_all[col, :, :, :, t * 16:(t + 1) * 16, :].astype(F32).reshape(32, 2, 8, 128)
            ar[col, :, t * 256:t * 256 + 128] = v[:, 0].reshape(256, 128).astype(BF)
            ar[col, :, t * 256 + 128:(t + 1) * 256] = v[:, 1].reshape(256, 128).astype(BF)
        part = nt_dot(ar[col], kva[col].reshape(128, 1024)).T
        for bb in range(4):
            ck_send[col, bb] = part[bb * 32:(bb + 1) * 32, :]
        for k in range(1, 4):
            send("ck", ck_send.at[col, plus(b_me[col], k)], ck_recv.at[col, b_me[col]], col * 4 + k, col * 4 + b_me[col], b_dev(col, k))
        ck_recv[col, b_me[col]] = ck_send[col, b_me[col]]
    turn_kc()
    for col in range(2):
        for so in range(8):
            arrived("w1_p", w1.at[col, so, 1 - core], col * 8 + so)
        part = jnp.dot(ar[col], w1[col].reshape(1024, 512), preferred_element_type=F32)
        for bb in range(4):
            cq_send[col, bb] = part[:, bb * 128:(bb + 1) * 128]
        for k in range(1, 4):
            send("cq", cq_send.at[col, plus(b_me[col], k)], cq_recv.at[col, b_me[col]], col * 4 + k, col * 4 + b_me[col], b_dev(col, k))
        cq_recv[col, b_me[col]] = cq_send[col, b_me[col]]

    for col in range(2):
        for k in range(1, 4):
            b2 = plus(b_me[col], k)
            arrived("ck", ck_recv.at[col, b2], col * 4 + b2)
    u = ck_recv[0, 0]
    for i in range(1, 8):
        u = u + ck_recv[i // 4, i % 4]
    low, high = u[0:16], u[16:32]
    cos, sin = tab_kq[0], tab_kq[1]
    kvq[x_hi, core, x_lo, y, 0:16, :] = (low * cos - high * sin).astype(BF)
    kvq[x_hi, core, x_lo, y, 16:32, :] = (high * cos + low * sin).astype(BF)
    own_q = kvq.at[x_hi, core, x_lo, y]
    for k in range(1, 4):
        send("kq_y", own_q, own_q, k, y, b_dev(0, k))

    for k in order:
        for col in range(2):
            share_w(col, k)

    for col in range(2):
        for so in range(8):
            arrived("w2_p", w2_row(col, so, 1 - core), col * 8 + so)

    def heads(s):
        part = jnp.dot(x_v[s], w2[s // 2, s % 2].reshape(1024, D), preferred_element_type=F32)
        acc[...] = part if s == 0 else acc[...] + part

    for s in range(4):
        heads(s)
    turn_kq()
    for s in range(4, 8):
        heads(s)
    share_kc()

    @pl.loop(0, 4)
    def _(m):
        rows = pl.ds(pl.multiple_of(m * 256, 256), 256)
        u = acc[rows, :]
        acc[rows, :] = u * tab_c[0, rows, :] + pltpu.roll(u, 64, 1) * tab_c[1, rows, :]

    for col in range(2):
        for k in range(1, 4):
            b2 = plus(b_me[col], k)
            arrived("cq", cq_recv.at[col, b2], col * 4 + b2)
    u = cq_recv[0, 0]
    for i in range(1, 8):
        u = u + cq_recv[i // 4, i % 4]
    qq[...] = (u * tab_q[0] + pltpu.roll(u, 64, 1) * tab_q[1]).astype(BF)

    share_kq()
    prepare(core)
    take_kc()
    prepare(1 - core)

    for i in range(4):
        q = acc[i * 256:(i + 1) * 256, :].astype(BF)
        wide = (i + 1) * 256
        s_anchor = jnp.where(ctx > 0, scores_of(q, keys[0]), -1e30)
        s_own = scores_of(q, keys[ctx, :, 0:wide])
        row = lax.broadcasted_iota(jnp.int32, (256, wide), 0) + i * 256
        col = lax.broadcasted_iota(jnp.int32, (256, wide), 1)
        s_own = jnp.where(row >= col, s_own, -1e30)
        _, total, out = attend([s_anchor, s_own], [values[0], values[ctx, 0:wide, :]])
        c_out[i * 256:(i + 1) * 256, :] = (out / total).astype(BF)

    for i in range(2):
        rows = slice(i * 128, (i + 1) * 128)
        q = qq[rows, :]
        part_m[rows, :], part_l[rows, :], part_o[rows, :] = attend(
            [scores_of(q, keys[b]) for b in range(4)], [values[b] for b in range(4)])

    take_kq()
    for b in range(4):
        kv = kvq[b // 2, b % 2].reshape(8, 32, 256)
        qkeys[:, b * 256:(b + 1) * 256] = jnp.concatenate(
            [kv[j, 0:16] for j in range(4)] + [kv[j, 16:32] for j in range(4)], axis=0)
        qvalues[b * 256:(b + 1) * 256, :] = kv[4:8].reshape(128, 256).T
    for i in range(2):
        rows = slice(i * 128, (i + 1) * 128)
        s_self = scores_of(qq[rows, :], qkeys[...])
        row = lax.broadcasted_iota(jnp.int32, (128, 1024), 0) + (ctx * 256 + i * 128)
        col = lax.broadcasted_iota(jnp.int32, (128, 1024), 1)
        s_self = jnp.where(row >= col, s_self, -1e30)
        _, total, out = attend([s_self], [qvalues[...]], (part_m[rows, :], part_l[rows, :], part_o[rows, :]))
        q_out[rows, :] = (out / total).astype(BF)

    for copy in started:
        copy.wait_send()


def layer(context_x, query_x, w_query, key_value_weight, by_row, by_column):
    any_spec = pl.BlockSpec(memory_space=pl.ANY)
    vmem = pl.BlockSpec(memory_space=pltpu.VMEM)
    return pl.pallas_call(
        layer_kernel,
        out_shape=[jax.ShapeDtypeStruct((CTX_ROWS, D), BF), jax.ShapeDtypeStruct((Q_ROWS, D), BF)],
        in_specs=[any_spec, vmem, any_spec, any_spec, any_spec, any_spec],
        out_specs=[vmem, vmem],
        scratch_shapes=[
            pltpu.VMEM((NS, CTX_ROWS, 1024), BF),
            pltpu.VMEM((8, 64, 512), BF),
            pltpu.VMEM((256, 1024), BF),
            pltpu.VMEM((4, 2, 4, 32, 256), BF),
            pltpu.VMEM((2, 4, 32, 1024), BF),
            pltpu.VMEM((4, 2, 4, 2, 32, 128), BF),
            pltpu.VMEM((2, 8, 2, 64, 512), BF),
            pltpu.VMEM((4, 2, 4, 2, 2, 64, 128), BF),
            pltpu.VMEM((2, 4, 64, 128), BF),
            pltpu.VMEM((2, 4, 64, 128), BF),
            pltpu.VMEM((4, 2, 64, 128), BF),
            pltpu.VMEM((2, 4, 2, 4, 64, 128), BF),
            pltpu.VMEM((2, Q_ROWS, 1024), BF),
            pltpu.VMEM((2, 4, 32, Q_ROWS), F32),
            pltpu.VMEM((2, 4, 32, Q_ROWS), F32),
            pltpu.VMEM((2, 4, Q_ROWS, 128), F32),
            pltpu.VMEM((2, 4, Q_ROWS, 128), F32),
            pltpu.VMEM((2, 2, 2, 4, 32, 1024), BF),
            pltpu.VMEM((2, 2, 2, 4, 32, 256), BF),
            pltpu.VMEM((CTX_ROWS, D), F32),
            pltpu.VMEM((Q_ROWS, D), BF),
            pltpu.VMEM((4, 128, 1024), BF),
            pltpu.VMEM((4, 1024, 128), BF),
            pltpu.VMEM((128, 1024), BF),
            pltpu.VMEM((1024, 128), BF),
            pltpu.VMEM((Q_ROWS, 1), F32),
            pltpu.VMEM((Q_ROWS, 1), F32),
            pltpu.VMEM((Q_ROWS, D), F32),
            pltpu.VMEM((2, CTX_ROWS, D), F32),
            pltpu.VMEM((2, Q_ROWS, D), F32),
            pltpu.VMEM((2, 16, 1024), F32),
            pltpu.VMEM((2, 16, 256), F32),
            pltpu.SemaphoreType.DMA((SLOTS,)),
            pltpu.SemaphoreType.DMA((SLOTS,)),
            pltpu.SemaphoreType.DMA((NS,)),
            pltpu.SemaphoreType.DMA((4,)),
            pltpu.SemaphoreType.DMA((3,)),
        ],
        compiler_params=pltpu.CompilerParams(
            collective_id=0, has_side_effects=True, vmem_limit_bytes=VMEM_LIMIT),
        name="layer",
    )(context_x, query_x, w_query, key_value_weight, by_row, by_column)


def finish_kernel(c_from, q_from, c_to, q_to):
    c_to[...] = c_from[...]
    q_to[...] = q_from[...]


def finish(c, q):
    return pl.pallas_call(
        finish_kernel,
        out_shape=[jax.ShapeDtypeStruct(c.shape, BF), jax.ShapeDtypeStruct(q.shape, BF)],
        name="finish",
    )(c, q)


def per_device(context_x, query_x, w_query, key_value_weight):
    by_row, by_column = rope_tables()
    return tuple(finish(*layer(
        context_x, query_x, w_query, key_value_weight, jnp.asarray(by_row), jnp.asarray(by_column))))


def solution(mesh):
    placed = (P("ctx", None), P(("ctx", "wt"), None), P("wt", None), P("wt", None))
    return jax.shard_map(
        per_device,
        mesh=mesh,
        in_specs=placed,
        out_specs=(P("ctx", "wt"), P("ctx", "wt")),
        check_vma=False,
    )
```

```python
import math

import jax
import jax.numpy as jnp
import numpy as np
from jax import lax
from jax.experimental import pallas as pl
from jax.experimental.pallas import tpu as pltpu
from jax.sharding import PartitionSpec as P


BF = jnp.bfloat16
F32 = jnp.float32
D = 128
NS, NY = 8, 4
CTX_ROWS = 1024
Q_ROWS = 256
TOKENS = 4096
POSITIONS = 5120
EXP2_SCALE = math.log2(math.e) / math.sqrt(D)
MESH = pl.DeviceIdType.MESH
VMEM_LIMIT = 56 * 1024 * 1024


def rope_tables():
    half = D // 2
    frequency = 500000.0 ** (-2.0 * np.arange(half) / D)
    angle = np.arange(POSITIONS)[:, None] * frequency[None, :]
    cos, sin = np.cos(angle), np.sin(angle)
    by_row = np.stack([np.concatenate([cos, cos], 1), np.concatenate([-sin, sin], 1)])
    shape = (1, 4, 16, POSITIONS)
    cos_t = np.concatenate([cos.T.reshape(shape), np.ones(shape)])
    sin_t = np.concatenate([sin.T.reshape(shape), np.zeros(shape)])
    return by_row.astype(np.float32), np.stack([cos_t, sin_t]).astype(np.float32)


def nt_dot(a, b):
    return lax.dot_general(a, b, (((1,), (1,)), ((), ())), preferred_element_type=F32)


SLOTS_OF = dict(kvd=32, kvd_p=4, kv1=16, kv1_p=2, w1=16, a1=16, a2=8, w1_p=16, w2=64, w2_p=16, ck=8, cq=8,
                kc_y=4, kc_x=4, kc_p=4, kq_y=4, kq_x=4, kq_p=1)
BASE = {}
SLOTS = 0
for _name, _count in SLOTS_OF.items():
    BASE[_name] = SLOTS
    SLOTS += _count


def scores_of(q, keys):
    return jnp.dot(q, keys, preferred_element_type=F32)


def attend(scores, values, before=None):
    top = jnp.max(scores[0], axis=1, keepdims=True)
    for s in scores[1:]:
        top = jnp.maximum(top, jnp.max(s, axis=1, keepdims=True))
    if before is not None:
        top = jnp.maximum(top, before[0])
    total = out = None
    for s, v in zip(scores, values):
        w = jnp.exp2((s - top) * EXP2_SCALE)
        t = jnp.sum(w, axis=1, keepdims=True)
        o = jnp.dot(w.astype(BF), v, preferred_element_type=F32)
        total, out = (t, o) if total is None else (total + t, out + o)
    if before is not None:
        shrink = jnp.exp2((before[0] - top) * EXP2_SCALE)
        total = total + before[1] * shrink
        out = out + before[2] * shrink
    return top, total, out


def layer_kernel(x_hbm, qx, wq_hbm, kvw_hbm, tabq_hbm, tabk_hbm, c_out, q_out,
                 x_v, w_src, kv_src, kvt, kva, kws, w1, w2, asend, a1_0, a1_1, a_all, ar,
                 ck_send, ck_recv, cq_send, cq_recv,
                 kvc, kvq, acc, qq, keys, values, qkeys, qvalues, part_m, part_l, part_o,
                 tab_c, tab_q, tab_kc, tab_kq, send_sem, recv_sem, x_sem, tab_sem, load_sem):
    ctx = lax.axis_index("ctx")
    wt = lax.axis_index("wt")
    x_hi, core = ctx // 2, lax.rem(ctx, 2)
    z, x_lo, y = wt // 8, lax.rem(wt // 4, 2), lax.rem(wt, 4)
    x_me = x_hi * 2 + x_lo
    partner = (x_hi * 2 + 1 - core, wt)
    o_me, b_me = (z, y), (y, z)
    so_me = (z * 2 + x_lo, y * 2 + x_lo)

    def plus(a, k):
        return lax.rem(a + k, 4)

    def device(c, z2, x2, y2):
        return (c, z2 * 8 + x2 * 4 + y2)

    def x_side(k):
        return x_lo if k % 2 == 0 else 1 - x_lo

    def so_at(col, k):
        return plus(o_me[col], k // 2) * 2 + x_side(k)

    def so_dev(col, k):
        c2 = ctx if k % 2 == 0 else lax.rem(x_hi + core, 2) * 2 + core
        o2 = plus(o_me[col], k // 2)
        return device(c2, o2, x_side(k), y) if col == 0 else device(c2, z, x_side(k), o2)

    def b_dev(col, k):
        return device(ctx, z, x_lo, plus(y, k)) if col == 0 else device(ctx, plus(z, k), x_lo, y)

    def o_dev(col, k):
        return b_dev(1 - col, k)

    def a1_dev(col, k):
        b2 = plus(b_me[col], k // 2)
        return device(ctx, z, x_side(k), b2) if col == 0 else device(ctx, b2, x_side(k), y)

    def a1_slot(col, x2, b2):
        return col * 8 + (x2 * 4 + b2 if col == 0 else b2 * 2 + x2)

    def a1_at(col, x2, b2):
        return a1_0.at[x2, b2] if col == 0 else a1_1.at[b2, x2]

    def wt_at(k):
        return plus(z, k // 8), x_side(k), plus(y, k // 2)

    def wt_dev(k):
        return device(ctx, *wt_at(k))

    def x_at(k):
        return plus(x_me, k)

    def x_dev(k):
        x2 = x_at(k)
        return device((x2 // 2) * 2 + core, z, lax.rem(x2, 2), y)

    def rcopy(name, src, dst, slot_send, slot_recv, dev):
        return pltpu.make_async_remote_copy(
            src_ref=src, dst_ref=dst, send_sem=send_sem.at[BASE[name] + slot_send],
            recv_sem=recv_sem.at[BASE[name] + slot_recv], device_id=dev, device_id_type=MESH)

    started = []

    def send(name, src, dst, slot_send, slot_recv, dev):
        copy = rcopy(name, src, dst, slot_send, slot_recv, dev)
        copy.start()
        started.append(copy)
        return copy

    def sent(copies):
        for copy in copies:
            copy.wait_send()
        started[:] = [c for c in started if not any(c is copy for copy in copies)]

    def arrived(name, dst, slot):
        rcopy(name, dst, dst, 0, slot, partner).wait_recv()

    def lanes(i, width=128):
        return pl.ds(pl.multiple_of(i * width, width), width)

    load_kv = pltpu.make_async_copy(kvw_hbm, kv_src, load_sem.at[0])
    load_kv.start()
    for o2 in range(4):
        for x2 in range(2):
            for z2 in range(4):
                pltpu.make_async_copy(
                    wq_hbm.at[pl.ds(pl.multiple_of(128 + core * 64, 64), 64), pl.ds((z2 * 8 + x2 * 4 + o2) * 128, 128)],
                    w_src.at[o2 * 2 + x2, :, z2 * 128:(z2 + 1) * 128], load_sem.at[1]).start()
    first_rows = pl.ds(pl.multiple_of(core * 64, 64), 64)
    own_w = pltpu.make_async_copy(wq_hbm.at[first_rows, lanes(so_me[0], 512)], w1.at[0, so_me[0], core], load_sem.at[2])
    own_w.start()
    ctx_rows = pl.ds(pl.multiple_of(ctx * 1024, 1024), 1024)
    query_rows = pl.ds(pl.multiple_of(TOKENS + ctx * 256, 256), 256)
    tabs = [
        pltpu.make_async_copy(tabk_hbm.at[:, x_lo, y, :, ctx_rows], tab_kc, tab_sem.at[2]),
        pltpu.make_async_copy(tabk_hbm.at[:, x_lo, y, :, query_rows], tab_kq, tab_sem.at[3]),
        pltpu.make_async_copy(tabq_hbm.at[:, ctx_rows], tab_c, tab_sem.at[0]),
        pltpu.make_async_copy(tabq_hbm.at[:, query_rows], tab_q, tab_sem.at[1]),
    ]
    x_loads = [
        pltpu.make_async_copy(x_hbm.at[:, pl.ds(s * 1024, 1024)], x_v.at[s], x_sem.at[s])
        for s in range(NS)
    ]

    barrier = pltpu.get_barrier_semaphore()
    peers = [partner] + [x_dev(k) for k in range(1, 4)]
    peers += [wt_dev(k) for k in range(1, 32)]
    for col in range(2):
        peers += [so_dev(col, k) for k in (1, 3, 5, 7)]
    for dev in peers:
        pl.semaphore_signal(barrier, inc=1, device_id=dev, device_id_type=MESH)
    for copy in x_loads + tabs:
        copy.start()

    f = qx[...].astype(F32)
    for col in range(2):
        for bb in range(4):
            for t in range(4):
                at = [t * 2048 + bb * 256, t * 2048 + 1024 + bb * 256] if col == 0 else [
                    bb * 2048 + t * 256 + 128, bb * 2048 + 1024 + t * 256 + 128]
                tile = jnp.concatenate([f[:, c:c + 128] for c in at], axis=0)
                asend[col, bb, t * 16:(t + 1) * 16, :] = tile.astype(BF)
    a1_0[x_lo, y] = asend[0, y]
    a1_1[z, x_lo] = asend[1, z]

    core_cols = pl.ds(pl.multiple_of(core * 16, 16), 16)
    other_cols = pl.ds(pl.multiple_of(16 - core * 16, 16), 16)

    load_kv.wait()
    for g in range(4):
        for x2 in range(2):
            by_col = kv_src[:, g * 256 + x2 * 128:g * 256 + (x2 + 1) * 128].T
            if x2 == 0:
                by_col = jnp.concatenate(
                    [by_col[at + 16 * yy:at + 16 * yy + 16] for yy in range(4) for at in (0, 64)], axis=0)
            kvt[g, x2] = by_col.reshape(4, 32, 256)
    pltpu.make_async_copy(w_src, w_src, load_sem.at[1]).wait()
    w1[1, so_me[1], core] = w_src[so_me[1]]
    kva[0, :, core_cols, lanes(so_me[0])] = kvt[z, x_lo, :, core_cols, 0:128]
    for g in range(4):
        kva[1, g, core_cols, lanes(so_me[1])] = kvt[g, x_lo, y, core_cols, 128:256]
    kws[z, x_lo, y, core] = kvt[z, x_lo, y, :, lanes(core)]
    pl.semaphore_wait(barrier, len(peers))

    def kv_piece(col, k):
        o2 = plus(o_me[col], k // 2)
        if col == 0:
            return kvt.at[o2, x_side(k), :, core_cols, 0:128]
        return kvt.at[:, x_side(k), o2, core_cols, 128:256]

    half_lanes = lanes(core)
    for k in range(1, 32):
        z2, x2, y2 = wt_at(k)
        send("kvd", kvt.at[z2, x2, y2, :, half_lanes], kws.at[z, x_lo, y, core], k, wt, wt_dev(k))
    for k in (2, 6, 3, 7, 4, 5, 1):
        for col in range(2):
            send("a1", asend.at[col, plus(b_me[col], k // 2)], a1_at(col, x_lo, b_me[col]), col * 8 + k,
                 a1_slot(col, x_lo, b_me[col]), a1_dev(col, k))

    def w_piece(col, k):
        if col == 0:
            return wq_hbm.at[first_rows, lanes(so_at(0, k), 512)]
        return w_src.at[so_at(1, k)]

    def w2_at(col, so, b, c):
        o2, x2 = so // 2, lax.rem(so, 2)
        return w2.at[o2, x2, b, 0, c] if col == 0 else w2.at[b, x2, o2, 1, c]

    def w2_row(col, so, c):
        o2, x2 = so // 2, lax.rem(so, 2)
        return w2.at[o2, x2, :, 0, c] if col == 0 else w2.at[:, x2, o2, 1, c]

    def forward_w(col, k):
        so = so_at(col, k)
        if k > 0:
            arrived("w1", w1.at[col, so, core], col * 8 + so)
        for m in range(1, 4):
            send("w2", w1.at[col, so, core, :, lanes(plus(b_me[col], m))], w2_at(col, so, b_me[col], core),
                 (col * 8 + k) * 4 + m, (col * 8 + so) * 4 + b_me[col], b_dev(col, m))
        send("w1_p", w1.at[col, so, core], w1.at[col, so, core], col * 8 + k, col * 8 + so, partner)
        w2_at(col, so, b_me[col], core)[...] = w1[col, so, core, :, lanes(b_me[col])]

    for k in (2, 6, 3, 7, 1, 4, 5):
        for col in range(2):
            send("w1", w_piece(col, k), w1.at[col, so_me[col], core], col * 8 + k, col * 8 + so_me[col], so_dev(col, k))
    own_w.wait()
    for col in range(2):
        forward_w(col, 0)

    for col in range(2):
        for k in range(1, 8):
            x2, b2 = x_side(k), plus(b_me[col], k // 2)
            arrived("a1", a1_at(col, x2, b2), a1_slot(col, x2, b2))
    rows_at = (lambda o2: a_all.at[0, o2], lambda o2: a_all.at[1, :, :, o2])
    for k in (1, 3, 2):
        send("a2", a1_0, rows_at[0](z), k, z, o_dev(0, k))
        send("a2", a1_1, rows_at[1](y), 4 + k, 4 + y, o_dev(1, k))
    a_all[0, z] = a1_0[...]
    for z2 in range(4):
        for x2 in range(2):
            a_all[1, z2, x2, y] = a1_1[z2, x2]

    for k in (2, 6, 3, 7, 4, 5, 1):
        for col in range(2):
            send("kv1", kv_piece(col, k), kva.at[col, :, core_cols, lanes(so_me[col])], col * 8 + k, col * 8 + so_me[col], so_dev(col, k))

    near = (0, 1, 3, 2)
    order = (0, 2, 6, 3, 7, 1, 4, 5)
    for dz in near:
        z2 = plus(z, dz)
        for k in range(8 * dz, 8 * dz + 8):
            if k > 0:
                _, x2, y2 = wt_at(k)
                arrived("kvd", kws.at[z2, x2, y2, core], z2 * 8 + x2 * 4 + y2)
        send("kvd_p", kws.at[z2, :, :, core], kws.at[z2, :, :, core], dz, z2, partner)
    for copy in x_loads + tabs:
        copy.wait()
    u = None
    for dz in near:
        z2 = plus(z, dz)
        arrived("kvd_p", kws.at[z2, :, :, 1 - core], z2)
        for x2 in range(2):
            kw = jnp.concatenate([kws[z2, x2, yy, h] for yy in range(4) for h in range(2)], axis=1)
            part = nt_dot(kw, x_v[z2 * 2 + x2])
            u = part if u is None else u + part
    low, high = u[0:16], u[16:32]
    cos, sin = tab_kc[0], tab_kc[1]
    kvc[x_hi, core, x_lo, y, 0:16, :] = (low * cos - high * sin).astype(BF)
    kvc[x_hi, core, x_lo, y, 16:32, :] = (high * cos + low * sin).astype(BF)

    own = kvc.at[x_hi, core, x_lo, y]
    for k in range(1, 4):
        send("kc_y", own, own, k, y, b_dev(0, k))
    for k in order[1:]:
        for col in range(2):
            forward_w(col, k)

    def turn_kc():
        for k in range(1, 4):
            arrived("kc_y", kvc.at[x_hi, core, x_lo, plus(y, k)], plus(y, k))
        row = kvc.at[x_hi, core, x_lo]
        for k in (2, 1, 3):
            send("kc_x", row, row, k, x_me, x_dev(k))
        send("kc_p", row, row, 0, x_me, partner)

    def share_kc():
        for k in (1, 3, 2):
            xs = x_at(k)
            row = kvc.at[xs // 2, core, lax.rem(xs, 2)]
            arrived("kc_x", row, xs)
            send("kc_p", row, row, k, xs, partner)

    def take_kc():
        for k in range(4):
            xs = x_at(k)
            arrived("kc_p", kvc.at[xs // 2, 1 - core, lax.rem(xs, 2)], xs)

    def prepare(c):
        for xh in range(2):
            kv = kvc[xh, c].reshape(8, 32, 1024)
            keys[xh * 2 + c] = jnp.concatenate(
                [kv[j, 0:16] for j in range(4)] + [kv[j, 16:32] for j in range(4)], axis=0)
            values[xh * 2 + c] = kv[4:8].reshape(128, 1024).T

    def turn_kq():
        for k in range(1, 4):
            arrived("kq_y", kvq.at[x_hi, core, x_lo, plus(y, k)], plus(y, k))
        row_y = kvq.at[x_hi, core, x_lo]
        for k in range(1, 4):
            send("kq_x", row_y, row_y, k, x_me, x_dev(k))

    def share_kq():
        for k in range(1, 4):
            xs = x_at(k)
            arrived("kq_x", kvq.at[xs // 2, core, lax.rem(xs, 2)], xs)
        send("kq_p", kvq.at[:, core], kvq.at[:, core], 0, 0, partner)

    def take_kq():
        arrived("kq_p", kvq.at[:, 1 - core], 0)

    def share_w(col, k):
        so = so_at(col, k)
        for m in range(1, 4):
            b2 = plus(b_me[col], m)
            arrived("w2", w2_at(col, so, b2, core), (col * 8 + so) * 4 + b2)
        send("w2_p", w2_row(col, so, core), w2_row(col, so, core), col * 8 + k, col * 8 + so, partner)

    turn_kc()

    for col in range(2):
        for k in range(1, 8):
            arrived("kv1", kva.at[col, :, core_cols, lanes(so_at(col, k))], col * 8 + so_at(col, k))
        send("kv1_p", kva.at[col, :, core_cols], kva.at[col, :, core_cols], col, col, partner)
    for col in range(2):
        arrived("kv1_p", kva.at[col, :, other_cols], col)
        for k in range(1, 4):
            o2 = plus(o_me[col], k)
            arrived("a2", rows_at[col](o2), col * 4 + o2)
        for t in range(4):
            v = a_all[col, :, :, :, t * 16:(t + 1) * 16, :].astype(F32).reshape(32, 2, 8, 128)
            ar[col, :, t * 256:t * 256 + 128] = v[:, 0].reshape(256, 128).astype(BF)
            ar[col, :, t * 256 + 128:(t + 1) * 256] = v[:, 1].reshape(256, 128).astype(BF)
        part = nt_dot(ar[col], kva[col].reshape(128, 1024)).T
        for bb in range(4):
            ck_send[col, bb] = part[bb * 32:(bb + 1) * 32, :]
        for k in range(1, 4):
            send("ck", ck_send.at[col, plus(b_me[col], k)], ck_recv.at[col, b_me[col]], col * 4 + k, col * 4 + b_me[col], b_dev(col, k))
        ck_recv[col, b_me[col]] = ck_send[col, b_me[col]]
    for col in range(2):
        for so in range(8):
            arrived("w1_p", w1.at[col, so, 1 - core], col * 8 + so)
        part = jnp.dot(ar[col], w1[col].reshape(1024, 512), preferred_element_type=F32)
        for bb in range(4):
            cq_send[col, bb] = part[:, bb * 128:(bb + 1) * 128]
        for k in range(1, 4):
            send("cq", cq_send.at[col, plus(b_me[col], k)], cq_recv.at[col, b_me[col]], col * 4 + k, col * 4 + b_me[col], b_dev(col, k))
        cq_recv[col, b_me[col]] = cq_send[col, b_me[col]]

    for col in range(2):
        for k in range(1, 4):
            b2 = plus(b_me[col], k)
            arrived("ck", ck_recv.at[col, b2], col * 4 + b2)
    u = ck_recv[0, 0]
    for i in range(1, 8):
        u = u + ck_recv[i // 4, i % 4]
    low, high = u[0:16], u[16:32]
    cos, sin = tab_kq[0], tab_kq[1]
    kvq[x_hi, core, x_lo, y, 0:16, :] = (low * cos - high * sin).astype(BF)
    kvq[x_hi, core, x_lo, y, 16:32, :] = (high * cos + low * sin).astype(BF)
    own_q = kvq.at[x_hi, core, x_lo, y]
    for k in range(1, 4):
        send("kq_y", own_q, own_q, k, y, b_dev(0, k))

    for k in order:
        for col in range(2):
            share_w(col, k)

    for col in range(2):
        for so in range(8):
            arrived("w2_p", w2_row(col, so, 1 - core), col * 8 + so)

    def heads(s):
        part = jnp.dot(x_v[s], w2[s // 2, s % 2].reshape(1024, D), preferred_element_type=F32)
        acc[...] = part if s == 0 else acc[...] + part

    for s in range(4):
        heads(s)
    turn_kq()
    share_kc()
    for s in range(4, 8):
        heads(s)

    @pl.loop(0, 4)
    def _(m):
        rows = pl.ds(pl.multiple_of(m * 256, 256), 256)
        u = acc[rows, :]
        acc[rows, :] = u * tab_c[0, rows, :] + pltpu.roll(u, 64, 1) * tab_c[1, rows, :]

    prepare(core)
    take_kc()
    prepare(1 - core)

    for i in range(4):
        if i == 2:
            share_kq()
        q = acc[i * 256:(i + 1) * 256, :].astype(BF)
        wide = (i + 1) * 256
        s_anchor = jnp.where(ctx > 0, scores_of(q, keys[0]), -1e30)
        s_own = scores_of(q, keys[ctx, :, 0:wide])
        row = lax.broadcasted_iota(jnp.int32, (256, wide), 0) + i * 256
        col = lax.broadcasted_iota(jnp.int32, (256, wide), 1)
        s_own = jnp.where(row >= col, s_own, -1e30)
        _, total, out = attend([s_anchor, s_own], [values[0], values[ctx, 0:wide, :]])
        c_out[i * 256:(i + 1) * 256, :] = (out / total).astype(BF)

    for col in range(2):
        for k in range(1, 4):
            b2 = plus(b_me[col], k)
            arrived("cq", cq_recv.at[col, b2], col * 4 + b2)
    u = cq_recv[0, 0]
    for i in range(1, 8):
        u = u + cq_recv[i // 4, i % 4]
    qq[...] = (u * tab_q[0] + pltpu.roll(u, 64, 1) * tab_q[1]).astype(BF)

    for i in range(2):
        rows = slice(i * 128, (i + 1) * 128)
        q = qq[rows, :]
        part_m[rows, :], part_l[rows, :], part_o[rows, :] = attend(
            [scores_of(q, keys[b]) for b in range(4)], [values[b] for b in range(4)])

    take_kq()
    for b in range(4):
        kv = kvq[b // 2, b % 2].reshape(8, 32, 256)
        qkeys[:, b * 256:(b + 1) * 256] = jnp.concatenate(
            [kv[j, 0:16] for j in range(4)] + [kv[j, 16:32] for j in range(4)], axis=0)
        qvalues[b * 256:(b + 1) * 256, :] = kv[4:8].reshape(128, 256).T
    for i in range(2):
        rows = slice(i * 128, (i + 1) * 128)
        s_self = scores_of(qq[rows, :], qkeys[...])
        row = lax.broadcasted_iota(jnp.int32, (128, 1024), 0) + (ctx * 256 + i * 128)
        col = lax.broadcasted_iota(jnp.int32, (128, 1024), 1)
        s_self = jnp.where(row >= col, s_self, -1e30)
        _, total, out = attend([s_self], [qvalues[...]], (part_m[rows, :], part_l[rows, :], part_o[rows, :]))
        q_out[rows, :] = (out / total).astype(BF)

    for copy in started:
        copy.wait_send()


def layer(context_x, query_x, w_query, key_value_weight, by_row, by_column):
    any_spec = pl.BlockSpec(memory_space=pl.ANY)
    vmem = pl.BlockSpec(memory_space=pltpu.VMEM)
    return pl.pallas_call(
        layer_kernel,
        out_shape=[jax.ShapeDtypeStruct((CTX_ROWS, D), BF), jax.ShapeDtypeStruct((Q_ROWS, D), BF)],
        in_specs=[any_spec, vmem, any_spec, any_spec, any_spec, any_spec],
        out_specs=[vmem, vmem],
        scratch_shapes=[
            pltpu.VMEM((NS, CTX_ROWS, 1024), BF),
            pltpu.VMEM((8, 64, 512), BF),
            pltpu.VMEM((256, 1024), BF),
            pltpu.VMEM((4, 2, 4, 32, 256), BF),
            pltpu.VMEM((2, 4, 32, 1024), BF),
            pltpu.VMEM((4, 2, 4, 2, 32, 128), BF),
            pltpu.VMEM((2, 8, 2, 64, 512), BF),
            pltpu.VMEM((4, 2, 4, 2, 2, 64, 128), BF),
            pltpu.VMEM((2, 4, 64, 128), BF),
            pltpu.VMEM((2, 4, 64, 128), BF),
            pltpu.VMEM((4, 2, 64, 128), BF),
            pltpu.VMEM((2, 4, 2, 4, 64, 128), BF),
            pltpu.VMEM((2, Q_ROWS, 1024), BF),
            pltpu.VMEM((2, 4, 32, Q_ROWS), F32),
            pltpu.VMEM((2, 4, 32, Q_ROWS), F32),
            pltpu.VMEM((2, 4, Q_ROWS, 128), F32),
            pltpu.VMEM((2, 4, Q_ROWS, 128), F32),
            pltpu.VMEM((2, 2, 2, 4, 32, 1024), BF),
            pltpu.VMEM((2, 2, 2, 4, 32, 256), BF),
            pltpu.VMEM((CTX_ROWS, D), F32),
            pltpu.VMEM((Q_ROWS, D), BF),
            pltpu.VMEM((4, 128, 1024), BF),
            pltpu.VMEM((4, 1024, 128), BF),
            pltpu.VMEM((128, 1024), BF),
            pltpu.VMEM((1024, 128), BF),
            pltpu.VMEM((Q_ROWS, 1), F32),
            pltpu.VMEM((Q_ROWS, 1), F32),
            pltpu.VMEM((Q_ROWS, D), F32),
            pltpu.VMEM((2, CTX_ROWS, D), F32),
            pltpu.VMEM((2, Q_ROWS, D), F32),
            pltpu.VMEM((2, 16, 1024), F32),
            pltpu.VMEM((2, 16, 256), F32),
            pltpu.SemaphoreType.DMA((SLOTS,)),
            pltpu.SemaphoreType.DMA((SLOTS,)),
            pltpu.SemaphoreType.DMA((NS,)),
            pltpu.SemaphoreType.DMA((4,)),
            pltpu.SemaphoreType.DMA((3,)),
        ],
        compiler_params=pltpu.CompilerParams(
            collective_id=0, has_side_effects=True, vmem_limit_bytes=VMEM_LIMIT),
        name="layer",
    )(context_x, query_x, w_query, key_value_weight, by_row, by_column)


def finish_kernel(c_from, q_from, c_to, q_to):
    c_to[...] = c_from[...]
    q_to[...] = q_from[...]


def finish(c, q):
    return pl.pallas_call(
        finish_kernel,
        out_shape=[jax.ShapeDtypeStruct(c.shape, BF), jax.ShapeDtypeStruct(q.shape, BF)],
        name="finish",
    )(c, q)


def per_device(context_x, query_x, w_query, key_value_weight):
    by_row, by_column = rope_tables()
    return tuple(finish(*layer(
        context_x, query_x, w_query, key_value_weight, jnp.asarray(by_row), jnp.asarray(by_column))))


def solution(mesh):
    placed = (P("ctx", None), P(("ctx", "wt"), None), P("wt", None), P("wt", None))
    return jax.shard_map(
        per_device,
        mesh=mesh,
        in_specs=placed,
        out_specs=(P("ctx", "wt"), P("ctx", "wt")),
        check_vma=False,
    )
```
